128 devices in a mesh: row: 16 (over z_hi, y, core), col: 8 (over x, z_lo).
Axes of the slice: x: 4, y: 4, z: 4 (z_hi: 2, z_lo: 2; z = z_hi * 2 + z_lo), core: 2. Of those that a mesh axis runs over, the one named last changes fastest.
Arguments:
- amplitudes: bfloat16 [2, 16384, 2048], P(None, 'row', 'col'), may hold values from -6 to 6
- integrals: bfloat16 [2, 2048, 16384], P(None, 'row', 'col'), may hold values from -0.09375 to 0.09375
- tile_mask: int32 [2, 128, 16], P(None, 'row', 'col'), may hold values 0 or 1
- next_owner: int32 [16384, 1], P(('row', 'col')), may hold values from 0 to 127; in each aligned block of 128 rows (0 to 127, 128 to 255, ...) at most 2 rows name the same one
Outputs:
- relaid: bfloat16 [128, 256, 128, 128], P(('row', 'col'))
The draws below stay inside these ranges and needn't reach their ends.
Inputs may be any that keep to these rules, and one draw needn't show every extreme that they name: `next_owner`: among the 128 rows of one grid position, no owner is named more than 2 times, a bound that some block reaches.
All inputs are finite; a program needn't handle non-finite values. No bound on the sum of `tile_mask` on one device may be relied on, other than what follows from the above.
Results may differ from the reference program's by a relative error of at most 0.001.
Values may be sent and summed in bfloat16 or wider, within the bound.
No kernel may reach another device: no remote copies, remote signals or barrier semaphores. Data moves between devices by JAX's collectives and lax.ppermute only.
A program may use at most 128 MiB of HBM per device.

```python
import math
import jax
import jax.numpy as jnp
import numpy as np
from jax import lax

TILE = 128
PANELS = 2
MT_DEV = 8
NT_DEV = 16
M = 16384
N = 16384
KP = 2048
MT = 128
KPT = 16
TPD = 128
CAP = 2
SLOTS = 256
N_ROW = 16
N_COL = 8
DEVICES = 128


def touch_ends(entries, rng, least, high):
    dims = entries.shape
    index_at = [jax.random.randint(jax.random.fold_in(rng, axis), (), 0, dims[axis]) for axis in range(len(dims))]
    entries = entries.at[tuple(index_at)].set(least)
    longest = dims.index(max(dims))
    index_at[longest] = (index_at[longest] + 1) % dims[longest]
    return entries.at[tuple(index_at)].set(high)


def block_levels(own_key, extent, shards, smallest, top_value):
    def one(axis_at, blocks):
        draws = jax.random.uniform(jax.random.fold_in(jax.random.fold_in(own_key, 6), axis_at), (blocks,), jnp.float32, smallest / len(shards), top_value / len(shards))
        return jnp.repeat(jnp.exp(draws), extent[axis_at] // blocks).reshape((-1,) + (1,) * (len(extent) - axis_at - 1))

    factor_of = one(*shards[0])
    for cut in shards[1:]:
        factor_of = factor_of * one(*cut)
    return factor_of


def assign_block(rng, own, number, rows, amount, top, bound, skew):
    order = jax.random.permutation(rng, amount)
    packed, common = load_shares(amount, rows * top, bound, skew, True), load_shares(amount, rows * top, bound, skew, False)
    places = jnp.arange(amount)

    def named(tallies, offset_by):
        used = int((tallies > 0).sum())
        fixed = max(1, used // 4)
        passed = fixed + (places - fixed + offset_by * (used - fixed)) % max(1, amount - fixed)
        return jnp.zeros((amount,), jnp.int32).at[order[jnp.where(places < fixed, places, passed)]].set(jnp.asarray(tallies, jnp.int32))

    tallies = jnp.where(number % 4 == 0, named(packed, number // 4), named(common, number - number // 4 - 1))
    mixed = jax.random.permutation(jax.random.fold_in(own, 3), amount)
    giver, sink = mixed[0:amount // 2 * 2:2], mixed[1:amount // 2 * 2:2]
    room = jnp.minimum(tallies[giver] - 1, bound - tallies[sink]) // 2
    room = jnp.where((giver == order[0]) | (sink == order[0]) | (tallies[sink] == 0), 0, jnp.maximum(room, 0))
    passed = jax.random.randint(jax.random.fold_in(own, 4), (amount // 2,), 0, 1 << 20) % (room + 1)
    tallies = tallies.at[giver].add(-passed).at[sink].add(passed)
    items = jnp.searchsorted(jnp.cumsum(tallies), jnp.arange(rows * top), side="right").astype(jnp.int32)
    table = items.reshape(top, rows).T
    table = table[jax.random.permutation(jax.random.fold_in(own, 1), rows)]
    offset_by = jax.random.randint(jax.random.fold_in(own, 2), (rows, 1), 0, top)
    return jnp.take_along_axis(table, (jnp.arange(top)[None, :] + offset_by) % top, axis=1)


def load_shares(number_of, total, most, lean, full):
    loads = [(1 << 20) // math.isqrt(rank ** lean) + 1 for rank in range(1, number_of + 1)]
    largest = most if full else min(most, max(-(-total // number_of), total * loads[0] // sum(loads)))
    least = 1 if total - largest >= number_of - 1 else 0
    given, surplus = [largest] + [least] * (number_of - 1), total - largest - least * (number_of - 1)
    while surplus > 0:
        candidates = [i for i in range(1, number_of) if given[i] < largest] or [i for i in range(1, number_of) if given[i] < most]
        pool, remaining = sum([loads[i] for i in candidates]), surplus
        for i in candidates:
            extra = min(most - given[i], max(1, remaining * loads[i] // pool), surplus)
            given[i] = given[i] + extra
            surplus = surplus - extra
    return np.array(given)


def centred(key, dims, deviation, limit, shards=(), held_as=jnp.bfloat16):
    result = deviation * jax.random.normal(key, dims, jnp.float32)
    if shards:
        result = result * block_levels(key, dims, shards, -0.22, 0.18)
    return jnp.clip(result, -limit, limit).astype(held_as)


def setup_inputs(seed: int = 0) -> dict:
    splits = jax.random.split(jax.random.key(seed), 5)
    amplitudes = centred(splits[0], (PANELS, M, KP), 1.0, 6.0, ((1, 16), (2, 8)))
    integrals = centred(splits[1], (PANELS, KP, N), (PANELS * KP) ** -0.5, 0.09375, ((1, 16), (2, 8)))
    tile_mask = touch_ends((jax.random.randint(splits[2], (PANELS, MT, KPT), 0, 5) < 3).astype(jnp.int32), jax.random.fold_in(splits[2], 1), 0, 1)
    next_owner_keys = jax.random.split(jax.random.fold_in(splits[3], 1), (DEVICES * TPD) // TPD)
    next_owner_turns = jax.random.permutation(jax.random.fold_in(splits[3], 3), (DEVICES * TPD) // TPD)
    next_owner = jax.vmap(lambda own, number: assign_block(jax.random.fold_in(splits[3], 2), own, number, TPD, DEVICES, 1, CAP, 2))(next_owner_keys, next_owner_turns).reshape((DEVICES * TPD, 1))
    return {"amplitudes": amplitudes, "integrals": integrals, "tile_mask": tile_mask, "next_owner": next_owner}


def reference(amplitudes, integrals, tile_mask, next_owner):
    kept_tiles = tile_mask.astype(jnp.bfloat16)
    masked = amplitudes.reshape(PANELS, MT, TILE, KPT, TILE) * kept_tiles[:, :, None, :, None]
    masked = masked.reshape(PANELS, M, KP)

    def one_block(block_index):
        first_row = (block_index * (MT_DEV * TILE)).astype(jnp.int32)
        matched = lax.dynamic_slice_in_dim(masked, first_row, MT_DEV * TILE, 1)
        partial_value = jnp.dot(matched[0], integrals[0], preferred_element_type=jnp.float32)
        for panel_step in range(1, PANELS):
            partial_value = partial_value + jnp.dot(matched[panel_step], integrals[panel_step], preferred_element_type=jnp.float32)
        return partial_value.astype(jnp.bfloat16)

    result_slab = lax.map(one_block, jnp.arange(N_ROW, dtype=jnp.int32))
    result_tiles = result_slab.reshape(N_ROW, MT_DEV, TILE, N_COL, NT_DEV, TILE)
    result_tiles = result_tiles.transpose(0, 3, 1, 4, 2, 5).reshape(DEVICES, TPD, TILE, TILE)
    owners = next_owner.reshape(DEVICES, TPD)
    matches = (owners[:, :, None] == jnp.arange(DEVICES, dtype=jnp.int32)[None, None, :]).astype(jnp.int32)
    ranking = jnp.sum((jnp.cumsum(matches, axis=1) - 1) * matches, axis=2)
    slot_index = jnp.arange(DEVICES, dtype=jnp.int32)[:, None] * CAP + ranking
    relaid = jnp.zeros((DEVICES, SLOTS, TILE, TILE), jnp.bfloat16)
    return relaid.at[owners, slot_index].set(result_tiles)
```

```python
import jax
import jax.numpy as jnp
from jax import lax
from jax.experimental import pallas as pl
from jax.experimental.pallas import tpu as pltpu
from jax.sharding import PartitionSpec as P

TILE = 128
AXES = ("row", "col")
ROWS, COLS, DEPTH = 1024, 2048, 256
CHUNKS = 8
WIDE = 512
SLOTS = 256


def index_of(x, y, z, core):
    return ((z // 2) * 8 + y * 2 + core) * 8 + x * 2 + z % 2


def pairs(move):
    found = []
    for row in range(16):
        for col in range(8):
            place = (col // 2, (row // 2) % 4, (row // 8) * 2 + col % 2, row % 2)
            found.append((row * 8 + col, index_of(*move(*place))))
    return found


def along_x(step):
    return pairs(lambda x, y, z, core: ((x + step) % 4, y, z, core))


def along_y(step):
    return pairs(lambda x, y, z, core: (x, (y + step) % 4, z, core))


def across_z(bit):
    return pairs(lambda x, y, z, core: (x, y, z ^ bit, core))


def mate():
    return pairs(lambda x, y, z, core: (x, y, z, 1 - core))


def send(value, where):
    return lax.ppermute(value, AXES, where)


def mask_kernel(mask_ref, a_ref, out_ref):
    for panel in range(2):
        for i in range(ROWS // TILE):
            for k in range(DEPTH // TILE):
                at = (panel, pl.ds(i * TILE, TILE), pl.ds(k * TILE, TILE))
                kept = mask_ref[(panel * 8 + i) * 2 + k] != 0
                block = a_ref[at]
                out_ref[at] = jnp.where(kept, block, jnp.zeros_like(block))


def apply_mask(amplitudes, tile_mask):
    return pl.pallas_call(
        mask_kernel,
        out_shape=jax.ShapeDtypeStruct(amplitudes.shape, amplitudes.dtype),
        in_specs=[
            pl.BlockSpec(memory_space=pltpu.SMEM),
            pl.BlockSpec(memory_space=pltpu.VMEM),
        ],
        out_specs=pl.BlockSpec(memory_space=pltpu.VMEM),
        compiler_params=pltpu.CompilerParams(vmem_limit_bytes=8 << 20),
        cost_estimate=pl.CostEstimate(flops=0, bytes_accessed=2 << 20, transcendentals=0),
    )(tile_mask.reshape(-1), amplitudes)


def contract_kernel(place_ref, slot_ref, source_ref, *refs):
    (own_a, z_a, xm_a, xp_a, cm_a, cp_a, dm_a, dp_a) = refs[:8]
    b_here, b_mate = refs[8:17], refs[17:26]
    out_ref = refs[26]
    a_all, b_all, tiles, zero, a_sem, b_sem, out_sem = refs[27:]
    x, z_lo, y, z_hi, core = (place_ref[i] for i in range(5))

    def chunk_a(dx, dz):
        return ((x + dx) % 4) * 2 + jnp.bitwise_xor(z_lo, dz)

    def chunk_b(dy, dz):
        return jnp.bitwise_xor(z_hi, dz) * 4 + (y + dy) % 4

    plan_a = []
    for ref, dx, dz in ((own_a, 0, 0), (z_a, 0, 1), (xm_a, 3, 0), (xp_a, 1, 0), (cm_a, 3, 1), (cp_a, 1, 1)):
        plan_a += [(ref, 0, chunk_a(dx, dz), 0), (ref, 1, chunk_a(dx, dz), 1)]
    plan_a += [(cm_a, 2, chunk_a(2, 0), 0), (cp_a, 2, chunk_a(2, 0), 1)]
    plan_a += [(dm_a, 0, chunk_a(2, 1), 0), (dp_a, 0, chunk_a(2, 1), 1)]
    where_b = ((0, 0), (3, 0), (1, 0), (2, 0), (0, 1), (3, 1), (1, 1), (2, 1), (2, 1))

    def b_copies(part):
        columns = pl.ds(part * WIDE, WIDE)
        for held, side in ((b_here, core), (b_mate, 1 - core)):
            for n, (dy, dz) in enumerate(where_b):
                chunk = chunk_b(dy, dz)
                depth = pl.ds(pl.multiple_of(side * TILE, TILE), TILE)
                for panel in range(2):
                    if n >= 7 and panel != n - 7:
                        continue
                    yield pltpu.make_async_copy(
                        held[n].at[0 if n >= 7 else panel, :, columns],
                        b_all.at[part % 2, chunk, panel, depth, :],
                        b_sem.at[part % 2],
                    )

    for copy in b_copies(0):
        copy.start()
    for ref, panel_from, chunk, panel in plan_a:
        pltpu.make_async_copy(ref.at[panel_from], a_all.at[chunk, panel], a_sem).start()
    zero[...] = jnp.zeros_like(zero)

    def clear(slot, carry):
        @pl.when(source_ref[slot] < 0)
        def _():
            pltpu.make_async_copy(zero, out_ref.at[slot], out_sem).start()

        return carry

    lax.fori_loop(0, SLOTS, clear, 0)
    pltpu.make_async_copy(a_all, a_all, a_sem).wait()
    for part in range(COLS // WIDE):
        if part + 1 < COLS // WIDE:
            for copy in b_copies(part + 1):
                copy.start()
        held = b_all.at[part % 2]
        pltpu.make_async_copy(held, held, b_sem.at[part % 2]).wait()
        right = b_all[part % 2].reshape(CHUNKS * 2 * DEPTH, WIDE)

        def rows(i, carry):
            at = pl.ds(pl.multiple_of(i * 256, 256), 256)
            total = jnp.zeros((256, WIDE), jnp.float32)
            left = jnp.concatenate(
                [a_all[c, p, at, :] for c in range(CHUNKS) for p in range(2)], axis=1
            )
            total = jnp.dot(left, right, preferred_element_type=jnp.float32).astype(jnp.bfloat16)
            for di in range(2):
                for j in range(WIDE // TILE):
                    number = (i * 2 + di) * (COLS // TILE) + part * (WIDE // TILE) + j
                    tiles[number] = total[di * TILE : (di + 1) * TILE, j * TILE : (j + 1) * TILE]
                    pltpu.make_async_copy(tiles.at[number], out_ref.at[slot_ref[number]], out_sem).start()
            return carry

        lax.fori_loop(0, ROWS // 256, rows, 0)
    pltpu.make_async_copy(out_ref, out_ref, out_sem).wait()


def contract(place, slots, sources, a_parts, b_here, b_mate):
    return pl.pallas_call(
        contract_kernel,
        out_shape=jax.ShapeDtypeStruct((SLOTS, TILE, TILE), jnp.bfloat16),
        in_specs=[pl.BlockSpec(memory_space=pltpu.SMEM)] * 3 + [pl.BlockSpec(memory_space=pl.ANY)] * 26,
        out_specs=pl.BlockSpec(memory_space=pl.ANY),
        scratch_shapes=[
            pltpu.VMEM((CHUNKS, 2, ROWS, DEPTH), jnp.bfloat16),
            pltpu.VMEM((2, CHUNKS, 2, DEPTH, WIDE), jnp.bfloat16),
            pltpu.VMEM((128, TILE, TILE), jnp.bfloat16),
            pltpu.VMEM((TILE, TILE), jnp.bfloat16),
            pltpu.SemaphoreType.DMA(()),
            pltpu.SemaphoreType.DMA((2,)),
            pltpu.SemaphoreType.DMA(()),
        ],
        compiler_params=pltpu.CompilerParams(vmem_limit_bytes=40 << 20),
        cost_estimate=pl.CostEstimate(flops=2 * 1024 * 2048 * 4096, bytes_accessed=40 << 20, transcendentals=0),
    )(place, slots, sources, *a_parts, *b_here, *b_mate)


def after(value, *earlier):
    return lax.optimization_barrier((value, *earlier))[0]


def local(amplitudes, integrals, tile_mask, next_owner):
    row, col = lax.axis_index("row"), lax.axis_index("col")
    place = jnp.stack([col // 2, col % 2, (row // 2) % 4, row // 8, row % 2]).astype(jnp.int32)

    owners = next_owner[:, 0]
    before = jnp.arange(TILE)[None, :] < jnp.arange(TILE)[:, None]
    rank = jnp.sum(((owners[None, :] == owners[:, None]) & before).astype(jnp.int32), axis=1)
    slots = owners * 2 + rank
    tile_at = slots[None, :] == jnp.arange(SLOTS, dtype=jnp.int32)[:, None]
    sources = jnp.max(jnp.where(tile_at, jnp.arange(TILE, dtype=jnp.int32)[None, :], -1), axis=1)

    b = integrals
    a = apply_mask(amplitudes, tile_mask)
    b_ym, b_yp = send(b, along_y(1)), send(b, along_y(-1))
    a_xm, a_xp, a_z = send(a, along_x(1)), send(a, along_x(-1)), send(a, across_z(1))
    b_late = after(b, b_ym)
    b_z, b_y2 = send(b_late, across_z(2)), send(b_late, along_y(2))
    a_cm = send(jnp.concatenate([a_z, a_xm[:1]], axis=0), along_x(1))
    a_cp = send(jnp.concatenate([a_z, a_xp[1:]], axis=0), along_x(-1))
    b_zym, b_zyp = send(b_z, along_y(1)), send(b_z, along_y(-1))
    a_dm, a_dp = send(a_cm[:1], along_x(1)), send(a_cp[1:2], along_x(-1))
    b_em, b_ep = send(b_zym[:1], along_y(1)), send(b_zyp[1:], along_y(-1))

    b_here = (b, b_ym, b_yp, b_y2, b_z, b_zym, b_zyp, b_em, b_ep)
    b_mate = tuple(send(v, mate()) for v in b_here)
    outgoing = contract(place, slots, sources, (a, a_z, a_xm, a_xp, a_cm, a_cp, a_dm, a_dp), b_here, b_mate)
    arrived = lax.all_to_all(outgoing, AXES, split_axis=0, concat_axis=0, tiled=True)
    return arrived[None]


def solution(mesh):
    return jax.shard_map(
        local,
        mesh=mesh,
        in_specs=(
            P(None, "row", "col"),
            P(None, "row", "col"),
            P(None, "row", "col"),
            P(AXES, None),
        ),
        out_specs=P(AXES, None, None, None),
        check_vma=False,
    )
```

```python
import jax
import jax.numpy as jnp
from jax import lax
from jax.experimental import pallas as pl
from jax.experimental.pallas import tpu as pltpu
from jax.sharding import PartitionSpec as P

TILE = 128
AXES = ("row", "col")
ROWS, COLS, DEPTH = 1024, 2048, 256
UNITS = 16
HALF = UNITS // 2
WIDE = 512
SLOTS = 256
VMEM = pl.BlockSpec(memory_space=pltpu.VMEM)
SMEM = pl.BlockSpec(memory_space=pltpu.SMEM)
ANY = pl.BlockSpec(memory_space=pl.ANY)
HBM = pl.BlockSpec(memory_space=pltpu.HBM)


def index_of(x, y, z, core):
    return ((z // 2) * 8 + y * 2 + core) * 8 + x * 2 + z % 2


def pairs(move):
    found = []
    for row in range(16):
        for col in range(8):
            place = (col // 2, (row // 2) % 4, (row // 8) * 2 + col % 2, row % 2)
            found.append((row * 8 + col, index_of(*move(*place))))
    return found


def along_x(step):
    return pairs(lambda x, y, z, core: ((x + step) % 4, y, z, core))


def along_y(step):
    return pairs(lambda x, y, z, core: (x, (y + step) % 4, z, core))


def across_z(bit):
    return pairs(lambda x, y, z, core: (x, y, z ^ bit, core))


def mate():
    return pairs(lambda x, y, z, core: (x, y, z, 1 - core))


def send(value, where):
    return lax.ppermute(value, AXES, where)


def hbm(value):
    return pltpu.with_memory_space_constraint(value, pltpu.HBM)


def vmem(value):
    return pltpu.with_memory_space_constraint(value, pltpu.VMEM)


def mask_kernel(mask_ref, a_ref, out_ref):
    for panel in range(2):
        for i in range(ROWS // TILE):
            for k in range(DEPTH // TILE):
                at = (panel, pl.ds(i * TILE, TILE), pl.ds(k * TILE, TILE))
                kept = mask_ref[(panel * 8 + i) * 2 + k] != 0
                block = a_ref[at]
                out_ref[at] = jnp.where(kept, block, jnp.zeros_like(block))


def apply_mask(amplitudes, tile_mask):
    return pl.pallas_call(
        mask_kernel,
        out_shape=jax.ShapeDtypeStruct(amplitudes.shape, amplitudes.dtype),
        in_specs=[
            pl.BlockSpec(memory_space=pltpu.SMEM),
            pl.BlockSpec(memory_space=pltpu.VMEM),
        ],
        out_specs=pl.BlockSpec(memory_space=pltpu.VMEM),
        compiler_params=pltpu.CompilerParams(vmem_limit_bytes=8 << 20),
        cost_estimate=pl.CostEstimate(flops=0, bytes_accessed=2 << 20, transcendentals=0),
    )(tile_mask.reshape(-1), amplitudes)


ORDER = (
    (0, 0, 0), (3, 0, 0), (1, 0, 0), (2, 0, 0), (0, 1, 0), (0, 0, 1), (3, 0, 1), (1, 0, 1),
    (3, 1, 0), (1, 1, 0), (2, 1, 0), (2, 0, 1), (0, 1, 1), (3, 1, 1), (1, 1, 1), (2, 1, 1),
)
CAME = ((0, 0), (0, 1), (3, 0), (1, 0), (3, 1), (1, 1), (2, 0), (2, 1))


def homes():
    row, col = lax.axis_index("row"), lax.axis_index("col")
    x, z_lo, y, z_hi, core = col // 2, col % 2, (row // 2) % 4, row // 8, row % 2
    found = []
    for dx, dz in CAME:
        chunk = ((x + dx) % 4) * 2 + jnp.bitwise_xor(z_lo, dz)
        for side in range(2):
            key = (
                jnp.bitwise_xor(chunk // 4, z_hi) * 8
                + ((chunk % 4 - y + 4) % 4) * 2
                + jnp.bitwise_xor(core, side)
            )
            found.append(sum(jnp.where(key == z * 8 + y_off * 2 + other, n, 0) for n, (y_off, z, other) in enumerate(ORDER)))
    return jnp.stack(found).astype(jnp.int32)


def multiply(left_ref, pieces, held, held_sem, use):
    def fetch(part):
        columns = pl.ds(pl.multiple_of(part * WIDE, WIDE), WIDE)
        for n, (ref, first) in enumerate(pieces):
            pltpu.make_async_copy(
                ref.at[pl.ds(first, 2), :, columns], held.at[part % 2, pl.ds(2 * n, 2)], held_sem.at[part % 2]
            ).start()

    fetch(0)

    def step(part, carry):
        @pl.when(part + 1 < COLS // WIDE)
        def _():
            fetch(part + 1)

        here = held.at[part % 2]
        pltpu.make_async_copy(here, here, held_sem.at[part % 2]).wait()
        right = held[part % 2].reshape(HALF * DEPTH, WIDE)
        use(part, jnp.dot(left_ref[...], right, preferred_element_type=jnp.float32))
        return carry

    return lambda: lax.fori_loop(0, COLS // WIDE, step, 0)


def first_kernel(home_ref, *refs):
    own_a, z_a, xm_a, xp_a, zxm_a, zxp_a, fm_a, fp_a = refs[:8]
    own_b, ym_b, yp_b, y2_b, z_b, e1_b, a_all, total_ref, held, sem, held_sem = refs[8:]
    plan = [(ref, panel, n, panel) for n, ref in enumerate((own_a, z_a, xm_a, xp_a, zxm_a, zxp_a)) for panel in range(2)]
    plan += [(fm_a, 0, 6, 0), (fp_a, 0, 6, 1), (fm_a, 1, 7, 0), (fp_a, 1, 7, 1)]
    for ref, panel_there, n, panel in plan:
        for side in range(2):
            to = pl.multiple_of(home_ref[n * 2 + side] * DEPTH + panel * TILE, TILE)
            pltpu.make_async_copy(
                ref.at[panel_there, :, pl.ds(side * TILE, TILE)], a_all.at[:, pl.ds(to, TILE)], sem
            ).start()

    def use(part, value):
        total_ref[:, pl.ds(pl.multiple_of(part * WIDE, WIDE), WIDE)] = value

    pieces = ((own_b, 0), (ym_b, 0), (yp_b, 0), (y2_b, 0), (z_b, 0), (e1_b, 0), (e1_b, 2), (e1_b, 4))
    run = multiply(a_all.at[:, pl.ds(0, HALF * DEPTH)], pieces, held, held_sem, use)
    pltpu.make_async_copy(a_all, a_all, sem).wait()
    run()


def second_kernel(slot_ref, empty_ref, *refs):
    a_all, total_ref, zym_b, zyp_b, zy2_b, e2_b, zym_m, zyp_m, zy2_m, out_ref, held, held_sem = refs

    def use(part, value):
        columns = pl.ds(pl.multiple_of(part * WIDE, WIDE), WIDE)
        total = (total_ref[:, columns] + value).astype(jnp.bfloat16)
        for i in range(ROWS // TILE):
            for j in range(WIDE // TILE):
                number = i * (COLS // TILE) + part * (WIDE // TILE) + j
                out_ref[slot_ref[number]] = total[i * TILE : (i + 1) * TILE, j * TILE : (j + 1) * TILE]
                out_ref[empty_ref[number]] = jnp.zeros((TILE, TILE), jnp.bfloat16)

    pieces = ((zym_b, 0), (zyp_b, 0), (zy2_b, 0), (e2_b, 0), (e2_b, 2), (zym_m, 0), (zyp_m, 0), (zy2_m, 0))
    multiply(a_all.at[:, pl.ds(HALF * DEPTH, HALF * DEPTH)], pieces, held, held_sem, use)()


HELD = [pltpu.VMEM((2, 2 * HALF, TILE, WIDE), jnp.bfloat16)]


def first_product(home, a_parts, b_parts):
    return pl.pallas_call(
        first_kernel,
        out_shape=(
            jax.ShapeDtypeStruct((ROWS, UNITS * DEPTH), jnp.bfloat16),
            jax.ShapeDtypeStruct((ROWS, COLS), jnp.float32),
        ),
        in_specs=[SMEM] + [HBM] * 6 + [VMEM] * 2 + [HBM] * 6,
        out_specs=(VMEM, VMEM),
        scratch_shapes=[*HELD, pltpu.SemaphoreType.DMA(()), pltpu.SemaphoreType.DMA((2,))],
        compiler_params=pltpu.CompilerParams(vmem_limit_bytes=16 << 20),
        cost_estimate=pl.CostEstimate(flops=ROWS * COLS * 4096, bytes_accessed=1 << 20, transcendentals=0),
    )(home, *[hbm(v) for v in a_parts[:6]], *[vmem(v) for v in a_parts[6:]], *[hbm(v) for v in b_parts])


def second_product(slots, empties, a_all, total, b_parts):
    return pl.pallas_call(
        second_kernel,
        out_shape=jax.ShapeDtypeStruct((SLOTS, TILE, TILE), jnp.bfloat16),
        in_specs=[SMEM] * 2 + [VMEM] * 9,
        out_specs=VMEM,
        scratch_shapes=[*HELD, pltpu.SemaphoreType.DMA((2,))],
        compiler_params=pltpu.CompilerParams(vmem_limit_bytes=16 << 20),
        cost_estimate=pl.CostEstimate(flops=ROWS * COLS * 4096, bytes_accessed=1 << 20, transcendentals=0),
    )(slots, empties, vmem(a_all), vmem(total), *[vmem(v) for v in b_parts])


def write_kernel(arrived_ref, out_ref, sem):
    for part in range(8):
        at = pl.ds(part * (SLOTS // 8), SLOTS // 8)
        pltpu.make_async_copy(arrived_ref.at[at], out_ref.at[0, at], sem).start()
    pltpu.make_async_copy(out_ref, out_ref, sem).wait()


def write_out(arrived):
    return pl.pallas_call(
        write_kernel,
        out_shape=jax.ShapeDtypeStruct((1, SLOTS, TILE, TILE), jnp.bfloat16),
        in_specs=[VMEM],
        out_specs=ANY,
        scratch_shapes=[pltpu.SemaphoreType.DMA(())],
        compiler_params=pltpu.CompilerParams(vmem_limit_bytes=12 << 20),
    )(arrived)


def after(values, earlier):
    held = lax.optimization_barrier((tuple(values), tuple(earlier)))
    return held[0], held[1]


def local(amplitudes, integrals, tile_mask, next_owner):
    owners = next_owner[:, 0]
    before = jnp.arange(TILE)[None, :] < jnp.arange(TILE)[:, None]
    rank = jnp.sum(((owners[None, :] == owners[:, None]) & before).astype(jnp.int32), axis=1)
    slots = owners * 2 + rank
    every = jnp.arange(SLOTS, dtype=jnp.int32)
    empty = jnp.logical_not(jnp.any(slots[None, :] == every[:, None], axis=1))
    below = jnp.sum((empty[None, :] & (every[None, :] < every[:, None])).astype(jnp.int32), axis=1)
    pick = empty[None, :] & (below[None, :] == every[: SLOTS // 2, None])
    empties = jnp.sum(jnp.where(pick, every[None, :], 0), axis=1)
    home = homes()

    b = integrals
    a = apply_mask(amplitudes, tile_mask)
    b_ym, b_yp = send(b, along_y(1)), send(b, along_y(-1))
    a_xm, a_xp, a_z = send(a, along_x(1)), send(a, along_x(-1)), send(a, across_z(1))
    (b, a), (b_ym, b_yp, a_xm, a_xp, a_z) = after((b, a), (b_ym, b_yp, a_xm, a_xp, a_z))
    a_zxm, a_zxp = send(a_z, along_x(1)), send(a_z, along_x(-1))
    b_z, b_y2 = send(b, across_z(2)), send(b, along_y(2))
    e1 = send(jnp.concatenate([b, b_ym, b_yp], axis=0), mate())
    from_m = jnp.concatenate([a_xm[:1], a_zxm[:1]], axis=0)
    from_p = jnp.concatenate([a_xp[1:], a_zxp[1:]], axis=0)
    (from_m, from_p, b_z, b_y2), (a_xm, a_xp, a_zxm, a_zxp, e1, slots, empties, home) = after(
        (from_m, from_p, b_z, b_y2), (a_xm, a_xp, a_zxm, a_zxp, e1, slots, empties, home)
    )
    a_fm, a_fp = send(from_m, along_x(1)), send(from_p, along_x(-1))
    b_zym, b_zyp, b_zy2 = send(b_z, along_y(1)), send(b_z, along_y(-1)), send(b_y2, across_z(2))
    e2 = jnp.concatenate([b_y2, b_z], axis=0)
    (b_zym, b_zyp, b_zy2, e2), (a_fm, a_fp) = after((b_zym, b_zyp, b_zy2, e2), (a_fm, a_fp))
    late = (b_zym, b_zyp, b_zy2, *(send(v, mate()) for v in (e2, b_zym, b_zyp, b_zy2)))

    a_all, total = first_product(
        home, (a, a_z, a_xm, a_xp, a_zxm, a_zxp, a_fm, a_fp), (b, b_ym, b_yp, b_y2, b_z, e1)
    )
    outgoing = second_product(slots, empties, a_all, total, late)
    arrived = lax.all_to_all(outgoing, AXES, split_axis=0, concat_axis=0, tiled=True)
    return write_out(arrived)


def solution(mesh):
    return jax.shard_map(
        local,
        mesh=mesh,
        in_specs=(
            P(None, "row", "col"),
            P(None, "row", "col"),
            P(None, "row", "col"),
            P(AXES, None),
        ),
        out_specs=P(AXES, None, None, None),
        check_vma=False,
    )
```

```python
import functools

import jax
import jax.numpy as jnp
from jax import lax
from jax.experimental import pallas as pl
from jax.experimental.pallas import tpu as pltpu
from jax.sharding import PartitionSpec as P

TILE = 128
AXES = ("row", "col")
ROWS, COLS, DEPTH = 1024, 2048, 256
UNITS = 16
WIDE = 512
SLOTS = 256
VMEM = pl.BlockSpec(memory_space=pltpu.VMEM)
SMEM = pl.BlockSpec(memory_space=pltpu.SMEM)
ANY = pl.BlockSpec(memory_space=pl.ANY)
HBM = pl.BlockSpec(memory_space=pltpu.HBM)


def index_of(x, y, z, core):
    return ((z // 2) * 8 + y * 2 + core) * 8 + x * 2 + z % 2


def pairs(move):
    found = []
    for row in range(16):
        for col in range(8):
            place = (col // 2, (row // 2) % 4, (row // 8) * 2 + col % 2, row % 2)
            found.append((row * 8 + col, index_of(*move(*place))))
    return found


def along_x(step):
    return pairs(lambda x, y, z, core: ((x + step) % 4, y, z, core))


def along_y(step):
    return pairs(lambda x, y, z, core: (x, (y + step) % 4, z, core))


def across_z(bit):
    return pairs(lambda x, y, z, core: (x, y, z ^ bit, core))


def mate():
    return pairs(lambda x, y, z, core: (x, y, z, 1 - core))


def send(value, where):
    return lax.ppermute(value, AXES, where)


def hbm(value):
    return pltpu.with_memory_space_constraint(value, pltpu.HBM)


def vmem(value):
    return pltpu.with_memory_space_constraint(value, pltpu.VMEM)


def mask_kernel(mask_ref, a_ref, out_ref):
    for panel in range(2):
        for i in range(ROWS // TILE):
            for k in range(DEPTH // TILE):
                at = (panel, pl.ds(i * TILE, TILE), pl.ds(k * TILE, TILE))
                kept = mask_ref[(panel * 8 + i) * 2 + k] != 0
                block = a_ref[at]
                out_ref[at] = jnp.where(kept, block, jnp.zeros_like(block))


def apply_mask(amplitudes, tile_mask):
    return pl.pallas_call(
        mask_kernel,
        out_shape=jax.ShapeDtypeStruct(amplitudes.shape, amplitudes.dtype),
        in_specs=[
            pl.BlockSpec(memory_space=pltpu.SMEM),
            pl.BlockSpec(memory_space=pltpu.VMEM),
        ],
        out_specs=pl.BlockSpec(memory_space=pltpu.VMEM),
        compiler_params=pltpu.CompilerParams(vmem_limit_bytes=8 << 20),
        cost_estimate=pl.CostEstimate(flops=0, bytes_accessed=2 << 20, transcendentals=0),
    )(tile_mask.reshape(-1), amplitudes)


CAME = ((0, 0), (0, 1), (3, 0), (1, 0), (3, 1), (1, 1), (2, 0), (2, 1))
LAST = (6, 7)


def unit_of(n, side):
    row, col = lax.axis_index("row"), lax.axis_index("col")
    dx, dz = CAME[n]
    chunk = ((col // 2 + dx) % 4) * 2 + jnp.bitwise_xor(col % 2, dz)
    across = jnp.bitwise_xor(chunk // 4, row // 8)
    along = (chunk % 4 - (row // 2) % 4 + 4) % 4
    return jnp.bitwise_xor(row % 2, side) * 8 + across * 4 + along


def comes_last(unit):
    found = [unit_of(n, side) == unit for n in LAST for side in range(2)]
    return functools.reduce(jnp.logical_or, found)


def placed(plan, a_all, sem):
    for ref, panel_there, n, panel in plan:
        for side in range(2):
            to = pl.multiple_of(unit_of(n, side) * DEPTH + panel * TILE, TILE)
            yield pltpu.make_async_copy(
                ref.at[panel_there, :, pl.ds(side * TILE, TILE)], a_all.at[:, pl.ds(to, TILE)], sem
            )


def when(wanted, act):
    if wanted is None:
        act()
    else:
        pl.when(wanted)(act)


def add_shards(groups, b_refs, a_all, total_ref, held, sems, ready, use=None):
    conditions = [None if wanted is None else comes_last(unit) == wanted for unit, _, wanted in groups]
    spots, refs = [], iter(b_refs)
    for (unit, count, _), condition in zip(groups, conditions):
        spots += [(next(refs), condition) for _ in range(count)]

    def copies(part):
        columns = pl.ds(pl.multiple_of(part * WIDE, WIDE), WIDE)
        for n, (ref, condition) in enumerate(spots):
            yield condition, pltpu.make_async_copy(
                ref.at[:, :, columns], held.at[part % 2, pl.ds(2 * n, 2)], sems.at[part % 2, n]
            )

    def start(part):
        for condition, copy in copies(part):
            when(condition, copy.start)

    def step(part, carry):
        pl.when(part + 1 < COLS // WIDE)(lambda: start(part + 1))
        for condition, copy in copies(part):
            when(condition, copy.wait)
        columns = pl.ds(pl.multiple_of(part * WIDE, WIDE), WIDE)
        n = 0
        for (unit, count, _), condition in zip(groups, conditions):

            def add(unit=unit, count=count, n=n):
                right = held[part % 2, pl.ds(2 * n, 2 * count)].reshape(count * DEPTH, WIDE)
                left = a_all[:, pl.ds(unit * DEPTH, count * DEPTH)]
                total_ref[:, columns] += jnp.dot(left, right, preferred_element_type=jnp.float32)

            when(condition, add)
            n += count
        if use is not None:
            use(part, columns)
        return carry

    start(0)
    ready()
    lax.fori_loop(0, COLS // WIDE, step, 0)


def first_kernel(slot_ref, empty_ref, *refs):
    a_refs, b_refs = refs[:6], refs[6:11]
    a_all, total_ref, held, held_sems, sem = refs[11:]
    plan = [(ref, panel, n, panel) for n, ref in enumerate(a_refs) for panel in range(2)]
    for copy in placed(plan, a_all, sem):
        copy.start()

    def ready():
        total_ref[...] = jnp.zeros_like(total_ref)
        came = a_all.at[:, pl.ds(0, 12 * DEPTH)]
        pltpu.make_async_copy(came, came, sem).wait()

    add_shards(FIRST, b_refs, a_all, total_ref, held, held_sems, ready)


def second_kernel(*refs):
    b_refs = refs[2:5]
    a_all, total_ref, held, held_sems = refs[5:]
    add_shards(SECOND, b_refs, a_all, total_ref, held, held_sems, lambda: None)


def third_kernel(*refs):
    (fm_a, fp_a), b_refs = refs[:2], refs[4:17]
    a_all, total_ref, held, held_sems, sem = refs[17:]
    plan = [(fm_a, 0, 6, 0), (fp_a, 0, 6, 1), (fm_a, 1, 7, 0), (fp_a, 1, 7, 1)]
    for copy in placed(plan, a_all, sem):
        copy.start()

    def ready():
        came = a_all.at[:, pl.ds(0, 4 * DEPTH)]
        pltpu.make_async_copy(came, came, sem).wait()

    add_shards(THIRD, b_refs, a_all, total_ref, held, held_sems, ready)


def fourth_kernel(slot_ref, empty_ref, *refs):
    a_all, b_refs = refs[0], refs[2:5]
    out_ref, total_ref, held, held_sems = refs[5:]

    def use(part, columns):
        total = total_ref[:, columns].astype(jnp.bfloat16)
        for i in range(ROWS // TILE):
            for j in range(WIDE // TILE):
                number = i * (COLS // TILE) + part * (WIDE // TILE) + j
                out_ref[slot_ref[number]] = total[i * TILE : (i + 1) * TILE, j * TILE : (j + 1) * TILE]
                out_ref[empty_ref[number]] = jnp.zeros((TILE, TILE), jnp.bfloat16)

    add_shards(FOURTH, b_refs, a_all, total_ref, held, held_sems, lambda: None, use)


FIRST = tuple((n, 1, False) for n in range(5))
SECOND = tuple((5 + n, 1, False) for n in range(3))
THIRD = ((8, 5, None), *((n, 1, True) for n in range(8)))
FOURTH = ((13, 3, None),)


def scratch(groups):
    units = sum(count for _, count, _ in groups)
    return [pltpu.VMEM((2, 2 * units, TILE, WIDE), jnp.bfloat16), pltpu.SemaphoreType.DMA((2, units))]


def cost(units):
    return pl.CostEstimate(flops=2 * ROWS * COLS * DEPTH * units, bytes_accessed=1 << 20, transcendentals=0)


SUMS = (
    jax.ShapeDtypeStruct((ROWS, UNITS * DEPTH), jnp.bfloat16),
    jax.ShapeDtypeStruct((ROWS, COLS), jnp.float32),
)
PARAMS = pltpu.CompilerParams(vmem_limit_bytes=16 << 20)


def first_product(slots, empties, a_parts, b_parts):
    return pl.pallas_call(
        first_kernel,
        out_shape=SUMS,
        in_specs=[SMEM] * 2 + [HBM] * 11,
        out_specs=(VMEM, VMEM),
        scratch_shapes=[*scratch(FIRST), pltpu.SemaphoreType.DMA(())],
        compiler_params=PARAMS,
        cost_estimate=cost(5),
    )(slots, empties, *[hbm(v) for v in (*a_parts, *b_parts)])


def second_product(sums, b_parts):
    return pl.pallas_call(
        second_kernel,
        out_shape=SUMS,
        in_specs=[VMEM] * 5,
        out_specs=(VMEM, VMEM),
        input_output_aliases={0: 0, 1: 1},
        scratch_shapes=scratch(SECOND),
        compiler_params=PARAMS,
        cost_estimate=cost(4),
    )(*[vmem(v) for v in (*sums, *b_parts)])


def third_product(a_parts, sums, b_parts):
    return pl.pallas_call(
        third_kernel,
        out_shape=SUMS,
        in_specs=[HBM] * 2 + [VMEM] * 2 + [HBM] * 13,
        out_specs=(VMEM, VMEM),
        input_output_aliases={2: 0, 3: 1},
        scratch_shapes=[*scratch(THIRD), pltpu.SemaphoreType.DMA(())],
        compiler_params=PARAMS,
        cost_estimate=cost(5),
    )(*[hbm(v) for v in a_parts], *[vmem(v) for v in sums], *[hbm(v) for v in b_parts])


def fourth_product(slots, empties, sums, b_parts):
    return pl.pallas_call(
        fourth_kernel,
        out_shape=(jax.ShapeDtypeStruct((SLOTS, TILE, TILE), jnp.bfloat16), SUMS[1]),
        in_specs=[SMEM] * 2 + [VMEM] * 5,
        out_specs=(VMEM, VMEM),
        input_output_aliases={3: 1},
        scratch_shapes=scratch(FOURTH),
        compiler_params=PARAMS,
        cost_estimate=cost(5),
    )(slots, empties, *[vmem(v) for v in (*sums, *b_parts)])[0]


def forward_kernel(xm_a, zxm_a, xp_a, zxp_a, to_m, to_p, sem):
    for out_ref, panel, refs in ((to_m, 0, (xm_a, zxm_a)), (to_p, 1, (xp_a, zxp_a))):
        for n, ref in enumerate(refs):
            pltpu.make_async_copy(ref.at[panel], out_ref.at[n], sem).start()
    for out_ref in (to_m, to_p):
        pltpu.make_async_copy(out_ref, out_ref, sem).wait()


def forwarded(a_xm, a_zxm, a_xp, a_zxp):
    shape = jax.ShapeDtypeStruct((2, ROWS, DEPTH), jnp.bfloat16)
    return pl.pallas_call(
        forward_kernel,
        out_shape=(shape, shape),
        in_specs=[ANY] * 4,
        out_specs=(VMEM, VMEM),
        scratch_shapes=[pltpu.SemaphoreType.DMA(())],
        compiler_params=pltpu.CompilerParams(vmem_limit_bytes=8 << 20),
        cost_estimate=pl.CostEstimate(flops=0, bytes_accessed=4 << 20, transcendentals=0),
    )(a_xm, a_zxm, a_xp, a_zxp)


def write_kernel(arrived_ref, out_ref, sem):
    for part in range(8):
        at = pl.ds(part * (SLOTS // 8), SLOTS // 8)
        pltpu.make_async_copy(arrived_ref.at[at], out_ref.at[0, at], sem).start()
    pltpu.make_async_copy(out_ref, out_ref, sem).wait()


def write_out(arrived):
    return pl.pallas_call(
        write_kernel,
        out_shape=jax.ShapeDtypeStruct((1, SLOTS, TILE, TILE), jnp.bfloat16),
        in_specs=[VMEM],
        out_specs=ANY,
        scratch_shapes=[pltpu.SemaphoreType.DMA(())],
        compiler_params=pltpu.CompilerParams(vmem_limit_bytes=12 << 20),
    )(arrived)


def after(values, earlier):
    held = lax.optimization_barrier((tuple(values), tuple(earlier)))
    return held[0], held[1]


def local(amplitudes, integrals, tile_mask, next_owner):
    owners = next_owner[:, 0]
    before = jnp.arange(TILE)[None, :] < jnp.arange(TILE)[:, None]
    rank = jnp.sum(((owners[None, :] == owners[:, None]) & before).astype(jnp.int32), axis=1)
    slots = owners * 2 + rank
    every = jnp.arange(SLOTS, dtype=jnp.int32)
    empty = jnp.logical_not(jnp.any(slots[None, :] == every[:, None], axis=1))
    below = jnp.sum((empty[None, :] & (every[None, :] < every[:, None])).astype(jnp.int32), axis=1)
    pick = empty[None, :] & (below[None, :] == every[: SLOTS // 2, None])
    empties = jnp.sum(jnp.where(pick, every[None, :], 0), axis=1)
    b = integrals
    a = apply_mask(amplitudes, tile_mask)
    b_ym, b_yp = send(b, along_y(1)), send(b, along_y(-1))
    a_xm, a_xp, a_z = send(a, along_x(1)), send(a, along_x(-1)), send(a, across_z(1))
    (a_m,), _ = after((a_z,), (a_xm,))
    (a_p,), _ = after((a_z,), (a_xp,))
    a_zxm, a_zxp = send(a_m, along_x(1)), send(a_p, along_x(-1))
    (b_for_z,), _ = after((b,), (a_z,))
    (b_for_y,), _ = after((b,), (b_ym, b_yp))
    b_z, b_y2 = send(b_for_z, across_z(2)), send(b_for_y, along_y(2))
    onward_m, onward_p = forwarded(a_xm, a_zxm, a_xp, a_zxp)
    a_fm, a_fp = send(onward_m, along_x(1)), send(onward_p, along_x(-1))
    (b_for_y,), _ = after((b_z,), (b_y2,))
    b_zym, b_zyp, b_zy2 = send(b_for_y, along_y(1)), send(b_for_y, along_y(-1)), send(b_y2, across_z(2))
    early = (b, b_yp, b_y2, b_ym, b_z)
    sums = first_product(slots, empties, (a, a_z, a_xm, a_xp, a_zxm, a_zxp), early)
    held, sums = after((*early, b_zyp, b_zy2, b_zym), sums)
    early, late = held[:5], held[5:]
    early_mate, late_mate = [send(v, mate()) for v in early], [send(v, mate()) for v in late]
    sums = second_product(sums, late)
    sums = third_product((a_fm, a_fp), sums, (*early_mate, *early, *late))
    outgoing = fourth_product(slots, empties, sums, late_mate)
    arrived = lax.all_to_all(outgoing, AXES, split_axis=0, concat_axis=0, tiled=True)
    return write_out(arrived)


def solution(mesh):
    return jax.shard_map(
        local,
        mesh=mesh,
        in_specs=(
            P(None, "row", "col"),
            P(None, "row", "col"),
            P(None, "row", "col"),
            P(AXES, None),
        ),
        out_specs=P(AXES, None, None, None),
        check_vma=False,
    )
```

```python
import functools

import jax
import jax.numpy as jnp
from jax import lax
from jax.experimental import pallas as pl
from jax.experimental.pallas import tpu as pltpu
from jax.sharding import PartitionSpec as P

TILE = 128
AXES = ("row", "col")
ROWS, COLS, DEPTH = 1024, 2048, 256
UNITS = 16
WIDE = 512
SLOTS = 256
VMEM = pl.BlockSpec(memory_space=pltpu.VMEM)
SMEM = pl.BlockSpec(memory_space=pltpu.SMEM)
ANY = pl.BlockSpec(memory_space=pl.ANY)
HBM = pl.BlockSpec(memory_space=pltpu.HBM)


def index_of(x, y, z, core):
    return ((z // 2) * 8 + y * 2 + core) * 8 + x * 2 + z % 2


def pairs(move):
    found = []
    for row in range(16):
        for col in range(8):
            place = (col // 2, (row // 2) % 4, (row // 8) * 2 + col % 2, row % 2)
            found.append((row * 8 + col, index_of(*move(*place))))
    return found


def along_x(step):
    return pairs(lambda x, y, z, core: ((x + step) % 4, y, z, core))


def along_y(step):
    return pairs(lambda x, y, z, core: (x, (y + step) % 4, z, core))


def across_z(bit):
    return pairs(lambda x, y, z, core: (x, y, z ^ bit, core))


def mate():
    return pairs(lambda x, y, z, core: (x, y, z, 1 - core))


def send(value, where):
    return lax.ppermute(value, AXES, where)


def hbm(value):
    return pltpu.with_memory_space_constraint(value, pltpu.HBM)


def vmem(value):
    return pltpu.with_memory_space_constraint(value, pltpu.VMEM)


def mask_kernel(mask_ref, a_ref, out_ref):
    for panel in range(2):
        for i in range(ROWS // TILE):
            for k in range(DEPTH // TILE):
                at = (panel, pl.ds(i * TILE, TILE), pl.ds(k * TILE, TILE))
                kept = mask_ref[(panel * 8 + i) * 2 + k] != 0
                block = a_ref[at]
                out_ref[at] = jnp.where(kept, block, jnp.zeros_like(block))


def apply_mask(amplitudes, tile_mask):
    return pl.pallas_call(
        mask_kernel,
        out_shape=jax.ShapeDtypeStruct(amplitudes.shape, amplitudes.dtype),
        in_specs=[
            pl.BlockSpec(memory_space=pltpu.SMEM),
            pl.BlockSpec(memory_space=pltpu.VMEM),
        ],
        out_specs=pl.BlockSpec(memory_space=pltpu.VMEM),
        compiler_params=pltpu.CompilerParams(vmem_limit_bytes=8 << 20),
        cost_estimate=pl.CostEstimate(flops=0, bytes_accessed=2 << 20, transcendentals=0),
    )(tile_mask.reshape(-1), amplitudes)


CAME = ((0, 0), (0, 1), (3, 0), (1, 0), (3, 1), (1, 1), (2, 0), (2, 1))
LAST = (6, 7)


def unit_of(n, side):
    row, col = lax.axis_index("row"), lax.axis_index("col")
    dx, dz = CAME[n]
    chunk = ((col // 2 + dx) % 4) * 2 + jnp.bitwise_xor(col % 2, dz)
    across = jnp.bitwise_xor(chunk // 4, row // 8)
    along = (chunk % 4 - (row // 2) % 4 + 4) % 4
    return jnp.bitwise_xor(row % 2, side) * 8 + across * 4 + along


def comes_last(unit):
    found = [unit_of(n, side) == unit for n in LAST for side in range(2)]
    return functools.reduce(jnp.logical_or, found)


def placed(plan, a_all, sem):
    for ref, panel_there, n, panel in plan:
        for side in range(2):
            to = pl.multiple_of(unit_of(n, side) * DEPTH + panel * TILE, TILE)
            yield pltpu.make_async_copy(
                ref.at[panel_there, :, pl.ds(side * TILE, TILE)], a_all.at[:, pl.ds(to, TILE)], sem
            )


def when(wanted, act):
    if wanted is None:
        act()
    else:
        pl.when(wanted)(act)


def add_shards(groups, b_refs, a_all, total_ref, held, sems, ready, use=None):
    conditions = [None if wanted is None else comes_last(unit) == wanted for unit, _, wanted in groups]
    spots, refs = [], iter(b_refs)
    for (unit, count, _), condition in zip(groups, conditions):
        spots += [(next(refs), condition) for _ in range(count)]

    def copies(part):
        columns = pl.ds(pl.multiple_of(part * WIDE, WIDE), WIDE)
        for n, (ref, condition) in enumerate(spots):
            yield condition, pltpu.make_async_copy(
                ref.at[:, :, columns], held.at[part % 2, pl.ds(2 * n, 2)], sems.at[part % 2, n]
            )

    def start(part):
        for condition, copy in copies(part):
            when(condition, copy.start)

    def step(part, carry):
        pl.when(part + 1 < COLS // WIDE)(lambda: start(part + 1))
        for condition, copy in copies(part):
            when(condition, copy.wait)
        columns = pl.ds(pl.multiple_of(part * WIDE, WIDE), WIDE)
        n = 0
        for (unit, count, _), condition in zip(groups, conditions):

            def add(unit=unit, count=count, n=n):
                right = held[part % 2, pl.ds(2 * n, 2 * count)].reshape(count * DEPTH, WIDE)
                left = a_all[:, pl.ds(unit * DEPTH, count * DEPTH)]
                total_ref[:, columns] += jnp.dot(left, right, preferred_element_type=jnp.float32)

            when(condition, add)
            n += count
        if use is not None:
            use(part, columns)
        return carry

    start(0)
    ready()
    lax.fori_loop(0, COLS // WIDE, step, 0)


def first_kernel(slot_ref, empty_ref, *refs):
    a_refs, b_refs = refs[:6], refs[6:11]
    a_all, total_ref, held, held_sems, sem = refs[11:]
    plan = [(ref, panel, n, panel) for n, ref in enumerate(a_refs) for panel in range(2)]
    for copy in placed(plan, a_all, sem):
        copy.start()

    def ready():
        total_ref[...] = jnp.zeros_like(total_ref)
        came = a_all.at[:, pl.ds(0, 12 * DEPTH)]
        pltpu.make_async_copy(came, came, sem).wait()

    add_shards(FIRST, b_refs, a_all, total_ref, held, held_sems, ready)


def second_kernel(*refs):
    b_refs = refs[2:5]
    a_all, total_ref, held, held_sems = refs[5:]
    add_shards(SECOND, b_refs, a_all, total_ref, held, held_sems, lambda: None)


def third_kernel(*refs):
    (fm_a, fp_a), b_refs = refs[:2], refs[4:15]
    a_all, total_ref, held, held_sems, sem = refs[15:]
    plan = [(fm_a, 0, 6, 0), (fp_a, 0, 6, 1), (fm_a, 1, 7, 0), (fp_a, 1, 7, 1)]
    for copy in placed(plan, a_all, sem):
        copy.start()

    def ready():
        came = a_all.at[:, pl.ds(0, 4 * DEPTH)]
        pltpu.make_async_copy(came, came, sem).wait()

    add_shards(THIRD, b_refs, a_all, total_ref, held, held_sems, ready)


def fourth_kernel(slot_ref, empty_ref, *refs):
    a_all, b_refs = refs[0], refs[2:7]
    out_ref, total_ref, held, held_sems = refs[7:]

    def use(part, columns):
        total = total_ref[:, columns].astype(jnp.bfloat16)
        for i in range(ROWS // TILE):
            for j in range(WIDE // TILE):
                number = i * (COLS // TILE) + part * (WIDE // TILE) + j
                out_ref[slot_ref[number]] = total[i * TILE : (i + 1) * TILE, j * TILE : (j + 1) * TILE]
                out_ref[empty_ref[number]] = jnp.zeros((TILE, TILE), jnp.bfloat16)

    add_shards(FOURTH, b_refs, a_all, total_ref, held, held_sems, lambda: None, use)


FIRST = tuple((n, 1, False) for n in range(5))
SECOND = tuple((5 + n, 1, False) for n in range(3))
THIRD = ((8, 2, None), (11, 1, None), *((n, 1, True) for n in range(8)))
FOURTH = ((10, 1, None), (12, 4, None))


def scratch(groups):
    units = sum(count for _, count, _ in groups)
    return [pltpu.VMEM((2, 2 * units, TILE, WIDE), jnp.bfloat16), pltpu.SemaphoreType.DMA((2, units))]


def cost(units):
    return pl.CostEstimate(flops=2 * ROWS * COLS * DEPTH * units, bytes_accessed=1 << 20, transcendentals=0)


SUMS = (
    jax.ShapeDtypeStruct((ROWS, UNITS * DEPTH), jnp.bfloat16),
    jax.ShapeDtypeStruct((ROWS, COLS), jnp.float32),
)
PARAMS = pltpu.CompilerParams(vmem_limit_bytes=16 << 20)


def first_product(slots, empties, a_parts, b_parts):
    return pl.pallas_call(
        first_kernel,
        out_shape=SUMS,
        in_specs=[SMEM] * 2 + [HBM] * 4 + [VMEM] * 2 + [HBM] * 5,
        out_specs=(VMEM, VMEM),
        scratch_shapes=[*scratch(FIRST), pltpu.SemaphoreType.DMA(())],
        compiler_params=PARAMS,
        cost_estimate=cost(5),
    )(slots, empties, *[hbm(v) for v in a_parts[:4]], *[vmem(v) for v in a_parts[4:]], *[hbm(v) for v in b_parts])


def second_product(sums, b_parts):
    return pl.pallas_call(
        second_kernel,
        out_shape=SUMS,
        in_specs=[VMEM] * 5,
        out_specs=(VMEM, VMEM),
        input_output_aliases={0: 0, 1: 1},
        scratch_shapes=scratch(SECOND),
        compiler_params=PARAMS,
        cost_estimate=cost(4),
    )(*[vmem(v) for v in (*sums, *b_parts)])


def third_product(a_parts, sums, b_parts):
    return pl.pallas_call(
        third_kernel,
        out_shape=SUMS,
        in_specs=[HBM] * 2 + [VMEM] * 5 + [HBM] * 8,
        out_specs=(VMEM, VMEM),
        input_output_aliases={2: 0, 3: 1},
        scratch_shapes=[*scratch(THIRD), pltpu.SemaphoreType.DMA(())],
        compiler_params=PARAMS,
        cost_estimate=cost(5),
    )(*[hbm(v) for v in a_parts], *[vmem(v) for v in (*sums, *b_parts[:3])], *[hbm(v) for v in b_parts[3:]])


def fourth_product(slots, empties, sums, b_parts):
    return pl.pallas_call(
        fourth_kernel,
        out_shape=(jax.ShapeDtypeStruct((SLOTS, TILE, TILE), jnp.bfloat16), SUMS[1]),
        in_specs=[SMEM] * 2 + [VMEM] * 7,
        out_specs=(VMEM, VMEM),
        input_output_aliases={3: 1},
        scratch_shapes=scratch(FOURTH),
        compiler_params=PARAMS,
        cost_estimate=cost(5),
    )(slots, empties, *[vmem(v) for v in (*sums, *b_parts)])[0]


def forward_kernel(xm_a, zxm_a, xp_a, zxp_a, to_m, to_p, sem):
    for out_ref, panel, refs in ((to_m, 0, (xm_a, zxm_a)), (to_p, 1, (xp_a, zxp_a))):
        for n, ref in enumerate(refs):
            pltpu.make_async_copy(ref.at[panel], out_ref.at[n], sem).start()
    for out_ref in (to_m, to_p):
        pltpu.make_async_copy(out_ref, out_ref, sem).wait()


def forwarded(a_xm, a_zxm, a_xp, a_zxp):
    shape = jax.ShapeDtypeStruct((2, ROWS, DEPTH), jnp.bfloat16)
    return pl.pallas_call(
        forward_kernel,
        out_shape=(shape, shape),
        in_specs=[ANY] * 4,
        out_specs=(VMEM, VMEM),
        scratch_shapes=[pltpu.SemaphoreType.DMA(())],
        compiler_params=pltpu.CompilerParams(vmem_limit_bytes=8 << 20),
        cost_estimate=pl.CostEstimate(flops=0, bytes_accessed=4 << 20, transcendentals=0),
    )(a_xm, a_zxm, a_xp, a_zxp)


def write_kernel(arrived_ref, out_ref, sem):
    for part in range(8):
        at = pl.ds(part * (SLOTS // 8), SLOTS // 8)
        pltpu.make_async_copy(arrived_ref.at[at], out_ref.at[0, at], sem).start()
    pltpu.make_async_copy(out_ref, out_ref, sem).wait()


def write_out(arrived):
    return pl.pallas_call(
        write_kernel,
        out_shape=jax.ShapeDtypeStruct((1, SLOTS, TILE, TILE), jnp.bfloat16),
        in_specs=[VMEM],
        out_specs=ANY,
        scratch_shapes=[pltpu.SemaphoreType.DMA(())],
        compiler_params=pltpu.CompilerParams(vmem_limit_bytes=12 << 20),
    )(arrived)


def after(values, earlier):
    held = lax.optimization_barrier((tuple(values), tuple(earlier)))
    return held[0], held[1]


def local(amplitudes, integrals, tile_mask, next_owner):
    owners = next_owner[:, 0]
    before = jnp.arange(TILE)[None, :] < jnp.arange(TILE)[:, None]
    rank = jnp.sum(((owners[None, :] == owners[:, None]) & before).astype(jnp.int32), axis=1)
    slots = owners * 2 + rank
    every = jnp.arange(SLOTS, dtype=jnp.int32)
    empty = jnp.logical_not(jnp.any(slots[None, :] == every[:, None], axis=1))
    below = jnp.sum((empty[None, :] & (every[None, :] < every[:, None])).astype(jnp.int32), axis=1)
    pick = empty[None, :] & (below[None, :] == every[: SLOTS // 2, None])
    empties = jnp.sum(jnp.where(pick, every[None, :], 0), axis=1)
    b = integrals
    a = apply_mask(amplitudes, tile_mask)
    b_ym, b_yp = send(b, along_y(1)), send(b, along_y(-1))
    a_xm, a_xp, a_z = send(a, along_x(1)), send(a, along_x(-1)), send(a, across_z(1))
    (a_m,), _ = after((a_z,), (a_xm,))
    (a_p,), _ = after((a_z,), (a_xp,))
    a_zxm, a_zxp = send(a_m, along_x(1)), send(a_p, along_x(-1))
    (b_for_z,), _ = after((b,), (a_z,))
    (b_for_y,), _ = after((b,), (b_ym, b_yp))
    b_z, b_y2 = send(b_for_z, across_z(2)), send(b_for_y, along_y(2))
    onward_m, onward_p = forwarded(a_xm, a_zxm, a_xp, a_zxp)
    a_fm, a_fp = send(onward_m, along_x(1)), send(onward_p, along_x(-1))
    (b_for_y,), _ = after((b_z,), (b_y2,))
    b_zym, b_zyp, b_zy2 = send(b_for_y, along_y(1)), send(b_for_y, along_y(-1)), send(b_y2, across_z(2))
    early = (b, b_yp, b_y2, b_ym, b_z)
    sums = first_product(slots, empties, (a, a_z, a_xm, a_xp, a_zxm, a_zxp), early)
    held, sums = after((b, b_yp, b_ym, b_y2, b_z, b_zyp, b_zy2, b_zym), sums)
    early, late = (held[0], held[1], held[3], held[2], held[4]), held[5:]
    first_mates = [send(v, mate()) for v in held[:3]]
    sums = second_product(sums, late)
    rest, sums = after(held[3:], sums)
    last_mates = [send(v, mate()) for v in rest]
    sums = third_product((a_fm, a_fp), sums, (*first_mates, *early, *late))
    outgoing = fourth_product(slots, empties, sums, last_mates)
    arrived = lax.all_to_all(outgoing, AXES, split_axis=0, concat_axis=0, tiled=True)
    return write_out(arrived)


def solution(mesh):
    return jax.shard_map(
        local,
        mesh=mesh,
        in_specs=(
            P(None, "row", "col"),
            P(None, "row", "col"),
            P(None, "row", "col"),
            P(AXES, None),
        ),
        out_specs=P(AXES, None, None, None),
        check_vma=False,
    )
```

```python
import functools

import jax
import jax.numpy as jnp
from jax import lax
from jax.experimental import pallas as pl
from jax.experimental.pallas import tpu as pltpu
from jax.sharding import PartitionSpec as P

TILE = 128
AXES = ("row", "col")
ROWS, COLS, DEPTH = 1024, 2048, 256
UNITS = 16
WIDE = 512
SLOTS = 256
VMEM = pl.BlockSpec(memory_space=pltpu.VMEM)
SMEM = pl.BlockSpec(memory_space=pltpu.SMEM)
ANY = pl.BlockSpec(memory_space=pl.ANY)
HBM = pl.BlockSpec(memory_space=pltpu.HBM)


def index_of(x, y, z, core):
    return ((z // 2) * 8 + y * 2 + core) * 8 + x * 2 + z % 2


def pairs(move):
    found = []
    for row in range(16):
        for col in range(8):
            place = (col // 2, (row // 2) % 4, (row // 8) * 2 + col % 2, row % 2)
            found.append((row * 8 + col, index_of(*move(*place))))
    return found


def along_x(step):
    return pairs(lambda x, y, z, core: ((x + step) % 4, y, z, core))


def along_y(step):
    return pairs(lambda x, y, z, core: (x, (y + step) % 4, z, core))


def across_z(bit):
    return pairs(lambda x, y, z, core: (x, y, z ^ bit, core))


def mate():
    return pairs(lambda x, y, z, core: (x, y, z, 1 - core))


def send(value, where):
    return lax.ppermute(value, AXES, where)


def hbm(value):
    return pltpu.with_memory_space_constraint(value, pltpu.HBM)


def vmem(value):
    return pltpu.with_memory_space_constraint(value, pltpu.VMEM)


def mask_kernel(mask_ref, a_ref, out_ref):
    for panel in range(2):
        for i in range(ROWS // TILE):
            for k in range(DEPTH // TILE):
                at = (panel, pl.ds(i * TILE, TILE), pl.ds(k * TILE, TILE))
                kept = mask_ref[(panel * 8 + i) * 2 + k] != 0
                block = a_ref[at]
                out_ref[at] = jnp.where(kept, block, jnp.zeros_like(block))


def apply_mask(amplitudes, tile_mask):
    return pl.pallas_call(
        mask_kernel,
        out_shape=jax.ShapeDtypeStruct(amplitudes.shape, amplitudes.dtype),
        in_specs=[
            pl.BlockSpec(memory_space=pltpu.SMEM),
            pl.BlockSpec(memory_space=pltpu.VMEM),
        ],
        out_specs=pl.BlockSpec(memory_space=pltpu.VMEM),
        compiler_params=pltpu.CompilerParams(vmem_limit_bytes=8 << 20),
        cost_estimate=pl.CostEstimate(flops=0, bytes_accessed=2 << 20, transcendentals=0),
    )(tile_mask.reshape(-1), amplitudes)


CAME = ((0, 0), (0, 1), (3, 0), (1, 0), (3, 1), (1, 1), (2, 0), (2, 1))
LAST = (6, 7)


def unit_of(n, side):
    row, col = lax.axis_index("row"), lax.axis_index("col")
    dx, dz = CAME[n]
    chunk = ((col // 2 + dx) % 4) * 2 + jnp.bitwise_xor(col % 2, dz)
    across = jnp.bitwise_xor(chunk // 4, row // 8)
    along = (chunk % 4 - (row // 2) % 4 + 4) % 4
    return jnp.bitwise_xor(row % 2, side) * 8 + across * 4 + along


def comes_last(unit):
    found = [unit_of(n, side) == unit for n in LAST for side in range(2)]
    return functools.reduce(jnp.logical_or, found)


def placed(plan, a_all, sem):
    for ref, panel_there, n, panel in plan:
        for side in range(2):
            to = pl.multiple_of(unit_of(n, side) * DEPTH + panel * TILE, TILE)
            yield pltpu.make_async_copy(
                ref.at[panel_there, :, pl.ds(side * TILE, TILE)], a_all.at[:, pl.ds(to, TILE)], sem
            )


def when(wanted, act):
    if wanted is None:
        act()
    else:
        pl.when(wanted)(act)


def add_shards(groups, b_refs, a_all, total_ref, held, sems, ready, use=None):
    conditions = [None if wanted is None else comes_last(unit) == wanted for unit, _, wanted in groups]
    spots, refs = [], iter(b_refs)
    for (unit, count, _), condition in zip(groups, conditions):
        spots += [(next(refs), condition) for _ in range(count)]

    def copies(part):
        columns = pl.ds(pl.multiple_of(part * WIDE, WIDE), WIDE)
        for n, (ref, condition) in enumerate(spots):
            yield condition, pltpu.make_async_copy(
                ref.at[:, :, columns], held.at[part % 2, pl.ds(2 * n, 2)], sems.at[part % 2, n]
            )

    def start(part):
        for condition, copy in copies(part):
            when(condition, copy.start)

    def step(part, carry):
        pl.when(part + 1 < COLS // WIDE)(lambda: start(part + 1))
        for condition, copy in copies(part):
            when(condition, copy.wait)
        columns = pl.ds(pl.multiple_of(part * WIDE, WIDE), WIDE)
        n = 0
        for (unit, count, _), condition in zip(groups, conditions):

            def add(unit=unit, count=count, n=n):
                right = held[part % 2, pl.ds(2 * n, 2 * count)].reshape(count * DEPTH, WIDE)
                left = a_all[:, pl.ds(unit * DEPTH, count * DEPTH)]
                total_ref[:, columns] += jnp.dot(left, right, preferred_element_type=jnp.float32)

            when(condition, add)
            n += count
        if use is not None:
            use(part, columns)
        return carry

    start(0)
    ready()
    lax.fori_loop(0, COLS // WIDE, step, 0)


def first_kernel(slot_ref, empty_ref, *refs):
    a_refs, b_refs = refs[:6], refs[6:12]
    a_all, total_ref, held, held_sems, sem = refs[12:]
    plan = [(ref, panel, n, panel) for n, ref in enumerate(a_refs) for panel in range(2)]
    for copy in placed(plan, a_all, sem):
        copy.start()

    def ready():
        total_ref[...] = jnp.zeros_like(total_ref)
        came = a_all.at[:, pl.ds(0, 12 * DEPTH)]
        pltpu.make_async_copy(came, came, sem).wait()

    add_shards(FIRST, b_refs, a_all, total_ref, held, held_sems, ready)


def second_kernel(*refs):
    b_refs = refs[2:5]
    a_all, total_ref, held, held_sems = refs[5:]
    add_shards(SECOND, b_refs, a_all, total_ref, held, held_sems, lambda: None)


def third_kernel(*refs):
    (fm_a, fp_a), b_refs = refs[:2], refs[4:15]
    a_all, total_ref, held, held_sems, sem = refs[15:]
    plan = [(fm_a, 0, 6, 0), (fp_a, 0, 6, 1), (fm_a, 1, 7, 0), (fp_a, 1, 7, 1)]
    for copy in placed(plan, a_all, sem):
        copy.start()

    def ready():
        came = a_all.at[:, pl.ds(0, 4 * DEPTH)]
        pltpu.make_async_copy(came, came, sem).wait()

    add_shards(THIRD, b_refs, a_all, total_ref, held, held_sems, ready)


def fourth_kernel(slot_ref, empty_ref, *refs):
    a_all, b_refs = refs[0], refs[2:7]
    out_ref, total_ref, held, held_sems = refs[7:]

    def use(part, columns):
        total = total_ref[:, columns].astype(jnp.bfloat16)
        for i in range(ROWS // TILE):
            for j in range(WIDE // TILE):
                number = i * (COLS // TILE) + part * (WIDE // TILE) + j
                out_ref[slot_ref[number]] = total[i * TILE : (i + 1) * TILE, j * TILE : (j + 1) * TILE]
                out_ref[empty_ref[number]] = jnp.zeros((TILE, TILE), jnp.bfloat16)

    add_shards(FOURTH, b_refs, a_all, total_ref, held, held_sems, lambda: None, use)


FIRST = tuple((n, 1, False) for n in (0, 1, 2, 3, 4, 8))
SECOND = tuple((5 + n, 1, False) for n in range(3))
THIRD = ((9, 1, None), (11, 1, None), *((n, 1, True) for n in range(9)))
FOURTH = ((10, 1, None), (12, 4, None))


def scratch(groups):
    units = sum(count for _, count, _ in groups)
    return [pltpu.VMEM((2, 2 * units, TILE, WIDE), jnp.bfloat16), pltpu.SemaphoreType.DMA((2, units))]


def cost(units):
    return pl.CostEstimate(flops=2 * ROWS * COLS * DEPTH * units, bytes_accessed=1 << 20, transcendentals=0)


SUMS = (
    jax.ShapeDtypeStruct((ROWS, UNITS * DEPTH), jnp.bfloat16),
    jax.ShapeDtypeStruct((ROWS, COLS), jnp.float32),
)
PARAMS = pltpu.CompilerParams(vmem_limit_bytes=16 << 20)


def first_product(slots, empties, a_parts, b_parts):
    return pl.pallas_call(
        first_kernel,
        out_shape=SUMS,
        in_specs=[SMEM] * 2 + [HBM] * 4 + [VMEM] * 2 + [HBM] * 6,
        out_specs=(VMEM, VMEM),
        scratch_shapes=[*scratch(FIRST), pltpu.SemaphoreType.DMA(())],
        compiler_params=PARAMS,
        cost_estimate=cost(5),
    )(slots, empties, *[hbm(v) for v in a_parts[:4]], *[vmem(v) for v in a_parts[4:]], *[hbm(v) for v in b_parts])


def second_product(sums, b_parts):
    return pl.pallas_call(
        second_kernel,
        out_shape=SUMS,
        in_specs=[VMEM] * 5,
        out_specs=(VMEM, VMEM),
        input_output_aliases={0: 0, 1: 1},
        scratch_shapes=scratch(SECOND),
        compiler_params=PARAMS,
        cost_estimate=cost(4),
    )(*[vmem(v) for v in (*sums, *b_parts)])


def third_product(a_parts, sums, b_parts):
    return pl.pallas_call(
        third_kernel,
        out_shape=SUMS,
        in_specs=[HBM] * 2 + [VMEM] * 4 + [HBM] * 9,
        out_specs=(VMEM, VMEM),
        input_output_aliases={2: 0, 3: 1},
        scratch_shapes=[*scratch(THIRD), pltpu.SemaphoreType.DMA(())],
        compiler_params=PARAMS,
        cost_estimate=cost(5),
    )(*[hbm(v) for v in a_parts], *[vmem(v) for v in (*sums, *b_parts[:2])], *[hbm(v) for v in b_parts[2:]])


def fourth_product(slots, empties, sums, b_parts):
    return pl.pallas_call(
        fourth_kernel,
        out_shape=(jax.ShapeDtypeStruct((SLOTS, TILE, TILE), jnp.bfloat16), SUMS[1]),
        in_specs=[SMEM] * 2 + [VMEM] * 7,
        out_specs=(VMEM, VMEM),
        input_output_aliases={3: 1},
        scratch_shapes=scratch(FOURTH),
        compiler_params=PARAMS,
        cost_estimate=cost(5),
    )(slots, empties, *[vmem(v) for v in (*sums, *b_parts)])[0]


def forward_kernel(xm_a, zxm_a, xp_a, zxp_a, to_m, to_p, sem):
    for out_ref, panel, refs in ((to_m, 0, (xm_a, zxm_a)), (to_p, 1, (xp_a, zxp_a))):
        for n, ref in enumerate(refs):
            pltpu.make_async_copy(ref.at[panel], out_ref.at[n], sem).start()
    for out_ref in (to_m, to_p):
        pltpu.make_async_copy(out_ref, out_ref, sem).wait()


def forwarded(a_xm, a_zxm, a_xp, a_zxp):
    shape = jax.ShapeDtypeStruct((2, ROWS, DEPTH), jnp.bfloat16)
    return pl.pallas_call(
        forward_kernel,
        out_shape=(shape, shape),
        in_specs=[ANY] * 4,
        out_specs=(VMEM, VMEM),
        scratch_shapes=[pltpu.SemaphoreType.DMA(())],
        compiler_params=pltpu.CompilerParams(vmem_limit_bytes=8 << 20),
        cost_estimate=pl.CostEstimate(flops=0, bytes_accessed=4 << 20, transcendentals=0),
    )(a_xm, a_zxm, a_xp, a_zxp)


def write_kernel(arrived_ref, out_ref, sem):
    for part in range(8):
        at = pl.ds(part * (SLOTS // 8), SLOTS // 8)
        pltpu.make_async_copy(arrived_ref.at[at], out_ref.at[0, at], sem).start()
    pltpu.make_async_copy(out_ref, out_ref, sem).wait()


def write_out(arrived):
    return pl.pallas_call(
        write_kernel,
        out_shape=jax.ShapeDtypeStruct((1, SLOTS, TILE, TILE), jnp.bfloat16),
        in_specs=[VMEM],
        out_specs=ANY,
        scratch_shapes=[pltpu.SemaphoreType.DMA(())],
        compiler_params=pltpu.CompilerParams(vmem_limit_bytes=12 << 20),
    )(arrived)


def after(values, earlier):
    held = lax.optimization_barrier((tuple(values), tuple(earlier)))
    return held[0], held[1]


def local(amplitudes, integrals, tile_mask, next_owner):
    owners = next_owner[:, 0]
    before = jnp.arange(TILE)[None, :] < jnp.arange(TILE)[:, None]
    rank = jnp.sum(((owners[None, :] == owners[:, None]) & before).astype(jnp.int32), axis=1)
    slots = owners * 2 + rank
    every = jnp.arange(SLOTS, dtype=jnp.int32)
    empty = jnp.logical_not(jnp.any(slots[None, :] == every[:, None], axis=1))
    below = jnp.sum((empty[None, :] & (every[None, :] < every[:, None])).astype(jnp.int32), axis=1)
    pick = empty[None, :] & (below[None, :] == every[: SLOTS // 2, None])
    empties = jnp.sum(jnp.where(pick, every[None, :], 0), axis=1)
    b = integrals
    own_mate = send(b, mate())
    a = apply_mask(amplitudes, tile_mask)
    (a,), (own_mate,) = after((a,), (own_mate,))
    b_ym, b_yp = send(b, along_y(1)), send(b, along_y(-1))
    a_xm, a_xp, a_z = send(a, along_x(1)), send(a, along_x(-1)), send(a, across_z(1))
    (a_m,), _ = after((a_z,), (a_xm,))
    (a_p,), _ = after((a_z,), (a_xp,))
    a_zxm, a_zxp = send(a_m, along_x(1)), send(a_p, along_x(-1))
    (b_for_z,), _ = after((b,), (a_z,))
    (b_for_y,), _ = after((b,), (b_ym, b_yp))
    b_z, b_y2 = send(b_for_z, across_z(2)), send(b_for_y, along_y(2))
    onward_m, onward_p = forwarded(a_xm, a_zxm, a_xp, a_zxp)
    a_fm, a_fp = send(onward_m, along_x(1)), send(onward_p, along_x(-1))
    (b_for_y,), _ = after((b_z,), (b_y2,))
    b_zym, b_zyp, b_zy2 = send(b_for_y, along_y(1)), send(b_for_y, along_y(-1)), send(b_y2, across_z(2))
    early = (b, b_yp, b_y2, b_ym, b_z)
    sums = first_product(slots, empties, (a, a_z, a_xm, a_xp, a_zxm, a_zxp), (*early, own_mate))
    held, sums = after((b, b_yp, b_ym, b_y2, b_z, b_zyp, b_zy2, b_zym), sums)
    early, late = (held[0], held[1], held[3], held[2], held[4]), held[5:]
    first_mates = [send(v, mate()) for v in held[1:3]]
    sums = second_product(sums, late)
    rest, sums = after(held[3:], sums)
    last_mates = [send(v, mate()) for v in rest]
    sums = third_product((a_fm, a_fp), sums, (*first_mates, *early, *late, own_mate))
    outgoing = fourth_product(slots, empties, sums, last_mates)
    arrived = lax.all_to_all(outgoing, AXES, split_axis=0, concat_axis=0, tiled=True)
    return write_out(arrived)


def solution(mesh):
    return jax.shard_map(
        local,
        mesh=mesh,
        in_specs=(
            P(None, "row", "col"),
            P(None, "row", "col"),
            P(None, "row", "col"),
            P(AXES, None),
        ),
        out_specs=P(AXES, None, None, None),
        check_vma=False,
    )
```
